128 devices in a mesh: pp: 2 (over y_hi), ep: 64 (over x, y_lo, z, core).
Axes of the slice: x: 4, y: 4 (y_hi: 2, y_lo: 2; y = y_hi * 2 + y_lo), z: 4, core: 2. Of those that a mesh axis runs over, the one named last changes fastest.
Arguments:
- entering: bfloat16 [2, 4096, 7168], P('pp', 'ep'), may hold values from -6 to 6
- norm_gain: float32 [2, 7168], P('pp'), may hold values from 0.1 to 1.9
- routes: int32 [2, 2, 4096, 2], P('pp', None, 'ep'), may hold values from 0 to 31, all different within a row; in each aligned block of 64 rows (0 to 63, 64 to 127, ..., all dimensions but the last counted through in order) at most 6 rows name the same one
- route_gates: float32 [2, 2, 4096, 2], P('pp', None, 'ep'), may hold values from 0.1 to 1
- w_gate: bfloat16 [2, 7168, 32768], P('pp', None, 'ep'), may hold values from -0.0625 to 0.0625
- w_up: bfloat16 [2, 7168, 32768], P('pp', None, 'ep'), may hold values from -0.0625 to 0.0625
- w_down: bfloat16 [2, 32768, 7168], P('pp', 'ep'), may hold values from -0.1875 to 0.1875
Outputs:
- finished: bfloat16 [2, 4096, 7168], P('pp', 'ep')
The draws below stay inside these ranges and needn't reach their ends.
Inputs may be any that keep to these rules, and one draw needn't show every extreme that they name: `routes`: each row names 2 different experts. In each aligned block of 64 rows of one layer and micro-batch (the rows of one device) no expert is named by more than 6 rows, a bound that some block reaches.
All inputs are finite; a program needn't handle non-finite values.
Results may differ from the reference program's by a relative error of at most 0.0075.
Values may be sent and summed in bfloat16 or wider, within the bound.
No kernel may reach another device: no remote copies, remote signals or barrier semaphores. Data moves between devices by JAX's collectives and lax.ppermute only.
A program may use at most 128 MiB of HBM per device.

```python
import math
import jax
import jax.numpy as jnp
import numpy as np
from jax import lax

D = 7168
FF = 1024
SHARDS = 2
TOPK = 2
TOK_DEV = 64
HID_DEV = 512
EXPERTS = 32
CAP = 6
TOKENS = 4096
HIDDEN_SIZE = 32768
N_EP = 64


def block_levels(stream_key, dims, cuts, low, high):
    gain = 1.0
    for axis_at, parts in cuts:
        draws = jax.random.uniform(jax.random.fold_in(jax.random.fold_in(stream_key, 6), axis_at), (parts,), jnp.float32, low / len(cuts), high / len(cuts))
        gain = gain * jnp.repeat(jnp.exp(draws), dims[axis_at] // parts).reshape((-1,) + (1,) * (len(dims) - 1 - axis_at))
    return gain


def routed_block(own_key, own, number, rows, number_of, top, most, skew):
    order = jax.random.permutation(own_key, number_of)
    heavy_load, ordinary = load_shares(number_of, rows * top, most, skew, True), load_shares(number_of, rows * top, most, skew, False)
    places = jnp.arange(number_of)

    def named(lengths, rotation):
        used = int((lengths > 0).sum())
        fixed = max(1, used // 4)
        moved = fixed + (places - fixed + rotation * (used - fixed)) % max(1, number_of - fixed)
        return jnp.zeros((number_of,), jnp.int32).at[order[jnp.where(places < fixed, places, moved)]].set(jnp.asarray(lengths, jnp.int32))

    lengths = jnp.where(number % 4 == 0, named(heavy_load, number // 4), named(ordinary, number - number // 4 - 1))
    mixed = jax.random.permutation(jax.random.fold_in(own, 3), number_of)
    source_of, receiver = mixed[0:number_of // 2 * 2:2], mixed[1:number_of // 2 * 2:2]
    room = jnp.minimum(lengths[source_of] - 1, most - lengths[receiver]) // 2
    room = jnp.where((source_of == order[0]) | (receiver == order[0]) | (lengths[receiver] == 0), 0, jnp.maximum(room, 0))
    moved = jax.random.randint(jax.random.fold_in(own, 4), (number_of // 2,), 0, 1 << 20) % (room + 1)
    lengths = lengths.at[source_of].add(-moved).at[receiver].add(moved)
    members = jnp.searchsorted(jnp.cumsum(lengths), jnp.arange(rows * top), side="right").astype(jnp.int32)
    grid = members.reshape(top, rows).T
    grid = grid[jax.random.permutation(jax.random.fold_in(own, 1), rows)]
    rotation = jax.random.randint(jax.random.fold_in(own, 2), (rows, 1), 0, top)
    return jnp.take_along_axis(grid, (jnp.arange(top)[None, :] + rotation) % top, axis=1)


def load_shares(amount, total, reach, lean, full):
    portions = [(1 << 20) // math.isqrt(rank ** lean) + 1 for rank in range(1, amount + 1)]
    largest = reach if full else min(reach, max(-(-total // amount), total * portions[0] // sum(portions)))
    least = 1 if total - largest >= amount - 1 else 0
    counts, surplus = [largest] + [least] * (amount - 1), total - largest - least * (amount - 1)
    while surplus > 0:
        candidates = [i for i in range(1, amount) if counts[i] < largest] or [i for i in range(1, amount) if counts[i] < reach]
        mass, budget = sum([portions[i] for i in candidates]), surplus
        for i in candidates:
            addition = min(reach - counts[i], max(1, budget * portions[i] // mass), surplus)
            counts[i] = counts[i] + addition
            surplus = surplus - addition
    return np.array(counts)


def bell_draw(rng, extent, deviation, most, pieces=(), held_as=jnp.bfloat16):
    level = block_levels(rng, extent, pieces, -0.22, 0.18) if pieces else 1.0
    array = jax.random.normal(rng, extent, jnp.float32) * deviation * level
    return jnp.minimum(jnp.maximum(array, -most), most).astype(held_as)


def setup_inputs(seed: int = 0) -> dict:
    seeds = jax.random.split(jax.random.key(seed), 8)
    entering = bell_draw(seeds[0], (2, TOKENS, D), 1.0, 6.0, ((0, 2), (1, 64)))
    norm_gain = jnp.clip(1.0 + 0.18 * jax.random.normal(seeds[1], (2, D), jnp.float32), 0.1, 1.9)
    routes_keys = jax.random.split(jax.random.fold_in(seeds[2], 1), 2 * 2 * TOKENS // TOK_DEV)
    routes_turns = jax.random.permutation(jax.random.fold_in(seeds[2], 3), 2 * 2 * TOKENS // TOK_DEV)
    routes = jax.vmap(lambda own, number: routed_block(jax.random.fold_in(seeds[2], 2), own, number, TOK_DEV, EXPERTS, TOPK, CAP, 2))(routes_keys, routes_turns).reshape((2, 2, TOKENS, TOPK))
    route_gates = jnp.clip(jnp.exp(math.log(1.0) - 2.3025851 * jax.random.uniform(seeds[3], (2, 2, TOKENS, TOPK), jnp.float32) ** block_levels(seeds[3], (2, 2, TOKENS, TOPK), ((0, 2), (2, 64)), -0.2, 0.2)), 0.1, 1.0)
    w_gate = bell_draw(seeds[4], (2, D, HIDDEN_SIZE), D ** -0.5, 0.0625, ((0, 2), (2, 64)))
    w_up = bell_draw(seeds[5], (2, D, HIDDEN_SIZE), D ** -0.5, 0.0625, ((0, 2), (2, 64)))
    w_down = bell_draw(seeds[6], (2, HIDDEN_SIZE, D), FF ** -0.5, 0.1875, ((0, 2), (1, 64)))
    return dict(entering=entering, norm_gain=norm_gain, routes=routes, route_gates=route_gates, w_gate=w_gate, w_up=w_up, w_down=w_down)


epsilon = 1e-06

def normalize(token_rows, gain_row):
    widened = token_rows.astype(jnp.float32)
    inv_rms = lax.rsqrt(lax.optimization_barrier(jnp.mean(widened * widened, axis=1, keepdims=True)) + epsilon)
    return (widened * inv_rms * gain_row.astype(jnp.float32)).astype(jnp.bfloat16)

def slot_numbers(chosen):
    flattened = chosen.reshape(-1)
    onehot = (flattened[:, None] == jnp.arange(EXPERTS, dtype=jnp.int32)[None, :]).astype(jnp.int32)
    before = jnp.cumsum(onehot, axis=0) - onehot
    return (flattened, lax.optimization_barrier(jnp.sum(before * onehot, axis=1)).astype(jnp.int32))

def moe_layer(token_rows, gain_row, chosen, pair_gates, w_gate, w_up, w_down):
    normed = normalize(token_rows, gain_row)
    flattened, slot_index = jax.vmap(slot_numbers)(chosen.reshape(N_EP, TOK_DEV, TOPK))
    column = (jnp.arange(N_EP, dtype=jnp.int32)[:, None] * CAP + slot_index).reshape(-1)
    flattened = flattened.reshape(-1)
    pair_token = jnp.arange(TOKENS * TOPK, dtype=jnp.int32) // TOPK
    source_ids = jnp.full((EXPERTS, N_EP * CAP), TOKENS, jnp.int32).at[flattened, column].set(pair_token)
    gate_table = jnp.zeros((EXPERTS, N_EP * CAP), jnp.float32).at[flattened, column].set(pair_gates.reshape(-1).astype(jnp.float32))
    padded = jnp.concatenate([normed, jnp.zeros((1, normed.shape[1]), normed.dtype)], axis=0)

    def one_expert(totals, expert):
        row_ids = lax.dynamic_index_in_dim(source_ids, expert, 0, keepdims=False)
        gathered = padded[row_ids]
        output = jnp.zeros((row_ids.shape[0], normed.shape[1]), jnp.float32)
        for shard in range(SHARDS):
            start = expert * FF + shard * HID_DEV
            gate_act = jnp.dot(gathered, lax.dynamic_slice_in_dim(w_gate, start, HID_DEV, 1), preferred_element_type=jnp.float32)
            up_act = jnp.dot(gathered, lax.dynamic_slice_in_dim(w_up, start, HID_DEV, 1), preferred_element_type=jnp.float32)
            hidden = (jax.nn.silu(gate_act) * up_act).astype(jnp.bfloat16)
            partial_value = jnp.dot(hidden, lax.dynamic_slice_in_dim(w_down, start, HID_DEV, 0), preferred_element_type=jnp.float32)
            output = output + lax.optimization_barrier(partial_value.astype(jnp.bfloat16)).astype(jnp.float32)
        output = lax.optimization_barrier(output.astype(jnp.bfloat16)).astype(jnp.float32)
        scaled = lax.dynamic_index_in_dim(gate_table, expert, 0, keepdims=False)[:, None] * output
        return (totals.at[row_ids].add(scaled), None)
    start_totals = jnp.zeros((TOKENS + 1, normed.shape[1]), jnp.float32)
    totals, ignored = lax.scan(one_expert, start_totals, jnp.arange(EXPERTS, dtype=jnp.int32))
    return (token_rows.astype(jnp.float32) + totals[:TOKENS]).astype(jnp.bfloat16)

def apply_layer(token_rows, layer_index, micro_batch, norm_gain, routes, route_gates, w_gate, w_up, w_down):
    return moe_layer(token_rows, norm_gain[layer_index], routes[layer_index, micro_batch], route_gates[layer_index, micro_batch], w_gate[layer_index], w_up[layer_index], w_down[layer_index])

def reference(entering, norm_gain, routes, route_gates, w_gate, w_up, w_down):
    params = (norm_gain, routes, route_gates, w_gate, w_up, w_down)
    moved_first = apply_layer(entering[0], 0, 0, *params)
    moved_second = apply_layer(entering[1], 1, 1, *params)
    finished_first = apply_layer(moved_second, 0, 1, *params)
    finished_second = apply_layer(moved_first, 1, 0, *params)
    return jnp.stack([finished_first, finished_second])
```

```python
import functools

import jax
import jax.numpy as jnp
import numpy as np
from jax import lax
from jax.experimental import pallas as pl
from jax.experimental.pallas import tpu as pltpu
from jax.sharding import PartitionSpec as P

EPS = 1e-06
SLOTS = 6
PARTS = 4
ROWS = SLOTS * PARTS
GROUP = 8
VMEM = 60 * 1024 * 1024

f32 = jnp.float32
bf16 = jnp.bfloat16


def spec(space=pltpu.VMEM):
    return pl.BlockSpec(memory_space=space)


def to_bf16(condition):
    return jnp.where(condition, 1.0, 0.0).astype(bf16)


def earlier_matrix(tokens):
    size = PARTS * tokens
    a, b = np.arange(size)[:, None], np.arange(size)[None, :]
    return ((a // tokens == b // tokens) & (a % tokens < b % tokens)).astype(jnp.bfloat16)


def order_matrix():
    size = GROUP * ROWS
    out = np.arange(size)
    q, rest = out // (GROUP * SLOTS), out % (GROUP * SLOTS)
    message, slot = rest // SLOTS, rest % SLOTS
    matrix = np.zeros((size, size), jnp.bfloat16)
    matrix[out, message * ROWS + q * SLOTS + slot] = 1
    return matrix


def selection(routes_ref, index, earlier_ref, tokens, experts):
    rows, columns = experts * ROWS, PARTS * tokens
    token = lax.broadcasted_iota(jnp.int32, (tokens, columns), 0)
    column = lax.broadcasted_iota(jnp.int32, (tokens, columns), 1)
    spread = to_bf16(token == lax.rem(column, tokens))
    chosen = routes_ref[index].astype(f32).astype(bf16)
    chosen = jnp.dot(chosen, spread, preferred_element_type=f32).astype(jnp.int32)
    row = lax.broadcasted_iota(jnp.int32, (rows, columns), 0)
    expert = lax.div(row, ROWS)
    rest = row - expert * ROWS
    piece = lax.div(rest, SLOTS)
    slot = rest - piece * SLOTS
    first = expert == chosen[0:1, :]
    named = jnp.logical_or(first, expert == chosen[1:2, :])
    before = jnp.dot(to_bf16(named), earlier_ref[...], preferred_element_type=f32)
    own = lax.div(lax.broadcasted_iota(jnp.int32, (rows, columns), 1), tokens)
    fits = jnp.logical_and(before.astype(jnp.int32) == slot, piece == own)
    return jnp.logical_and(named, fits), first


def put_normed(tokens_ref, gain_ref, stack_ref):
    tokens, width = tokens_ref.shape
    part = width // PARTS
    total = jnp.zeros((tokens, 1), f32)
    for q in range(PARTS):
        piece = tokens_ref[:, q * part : (q + 1) * part].astype(f32)
        total += jnp.sum(piece * piece, axis=1, keepdims=True)
    inverse = lax.rsqrt(total / width + EPS)
    for q in range(PARTS):
        piece = tokens_ref[:, q * part : (q + 1) * part].astype(f32)
        normed = piece * inverse * gain_ref[:, q * part : (q + 1) * part]
        stack_ref[q * tokens : (q + 1) * tokens, :] = normed.astype(bf16)


def put_packed(matrix, stack_ref, out_ref):
    out_ref[...] = jnp.dot(matrix, stack_ref[...], preferred_element_type=f32).astype(bf16)


def first_pack(experts, index_ref, tokens_ref, gain_ref, routes_ref, earlier_ref, out_ref, stack_ref):
    fills, _ = selection(routes_ref, index_ref[0], earlier_ref, tokens_ref.shape[0], experts)
    put_normed(tokens_ref, gain_ref, stack_ref)
    put_packed(to_bf16(fills), stack_ref, out_ref)


def second_pack(tokens_ref, gain_ref, send_ref, out_ref, stack_ref):
    put_normed(tokens_ref, gain_ref, stack_ref)
    put_packed(send_ref[...], stack_ref, out_ref)


def routing(experts, tokens, index_ref, routes_ref, gates_ref, earlier_ref, send_ref, *weights_refs):
    columns = PARTS * tokens
    token = lax.broadcasted_iota(jnp.int32, (tokens, columns), 0)
    column = lax.broadcasted_iota(jnp.int32, (tokens, columns), 1)
    spread = jnp.where(token == lax.rem(column, tokens), 1.0, 0.0)
    for stage in range(2):
        index = index_ref[stage]
        fills, first = selection(routes_ref, index, earlier_ref, tokens, experts)
        if stage == 1:
            send_ref[...] = to_bf16(fills)
        gates = jnp.dot(
            gates_ref[index], spread, preferred_element_type=f32, precision=lax.Precision.HIGHEST
        )
        scaled = jnp.where(fills, jnp.where(first, gates[0:1, :], gates[1:2, :]), 0.0).T
        high = scaled.astype(bf16)
        weights_refs[stage][0] = high
        weights_refs[stage][1] = (scaled - high.astype(f32)).astype(bf16)


def combine(tokens_ref, weights_ref, returned_ref, out_ref):
    tokens, width = tokens_ref.shape
    part = width // PARTS
    returned = returned_ref[...]
    for q in range(PARTS):
        rows = slice(q * tokens, (q + 1) * tokens)
        added = jnp.dot(weights_ref[0, rows, :], returned, preferred_element_type=f32)
        added += jnp.dot(weights_ref[1, rows, :], returned, preferred_element_type=f32)
        columns = slice(q * part, (q + 1) * part)
        out_ref[:, columns] = (tokens_ref[:, columns].astype(f32) + added).astype(bf16)


DEPTH = 3


def experts_kernel(
    arrived_ref, order_ref, back_ref, g0, u0, d0, g1, u1, d1, out_ref,
    stack_ref, first_buf, second_buf, act_ref, hidden_ref, result_ref, first_sem, second_sem,
):
    rows = stack_ref.shape[1]
    part = stack_ref.shape[2]
    half = g0.shape[1]
    groups = rows // (GROUP * SLOTS)
    size = GROUP * ROWS
    take = GROUP * SLOTS
    steps = [(gate, up, q) for gate, up in ((g0, u0), (g1, u1)) for q in range(PARTS)]

    def load_first(step):
        gate, up, q = steps[step]
        slot = step % DEPTH
        lines = pl.ds(q * part, part)
        return [
            pltpu.make_async_copy(
                source.at[lines, :], first_buf.at[slot, :, pl.ds(i * half, half)], first_sem.at[slot, i]
            )
            for i, source in enumerate((gate, up))
        ]

    def load_second(q):
        return [
            pltpu.make_async_copy(
                source.at[:, pl.ds(q * part, part)],
                second_buf.at[q, pl.ds(i * half, half), :],
                second_sem.at[q, i],
            )
            for i, source in enumerate((d0, d1))
        ]

    def start(copies):
        for copy in copies:
            copy.start()

    def wait(copies):
        for copy in copies:
            copy.wait()

    for step in range(DEPTH):
        start(load_first(step))
    for group in range(groups):
        moved = jnp.dot(
            order_ref[...], arrived_ref[group * size : (group + 1) * size, :], preferred_element_type=f32
        ).astype(bf16)
        for q in range(PARTS):
            stack_ref[q, group * take : (group + 1) * take, :] = moved[q * take : (q + 1) * take, :]
    for step in range(len(steps)):
        q = step % PARTS
        wait(load_first(step))
        product = jnp.dot(stack_ref[q], first_buf[step % DEPTH], preferred_element_type=f32)
        if q == 0:
            act_ref[...] = product
        else:
            act_ref[...] += product
        if step + DEPTH < len(steps):
            start(load_first(step + DEPTH))
        if step >= len(steps) - PARTS:
            start(load_second(step - len(steps) + PARTS))
        if q == PARTS - 1:
            gate = act_ref[:, :half]
            value = gate / (1.0 + jnp.exp(-gate)) * act_ref[:, half:]
            at = (step // PARTS) * half
            hidden_ref[:, at : at + half] = value.astype(bf16)
    for q in range(PARTS):
        wait(load_second(q))
        product = jnp.dot(hidden_ref[...], second_buf[q], preferred_element_type=f32).astype(bf16)
        for group in range(groups):
            result_ref[group, q * take : (q + 1) * take, :] = product[group * take : (group + 1) * take, :]
    for group in range(groups):
        out_ref[group * size : (group + 1) * size, :] = jnp.dot(
            back_ref[...], result_ref[group], preferred_element_type=f32
        ).astype(bf16)


def shards(entering, norm_gain, routes, route_gates, w_gate, w_up, w_down):
    section = lax.axis_index("pp")
    devices = lax.axis_size("ep")
    chips = devices // 2
    experts = chips
    own = entering[0]
    tokens, width = own.shape
    part = width // PARTS
    half = w_gate.shape[2]
    gain = norm_gain
    chosen = jnp.swapaxes(routes[0], 1, 2)
    gates = jnp.swapaxes(route_gates[0], 1, 2)
    order_of = jnp.stack([section, 1 - section]).astype(jnp.int32)
    earlier = jnp.asarray(earlier_matrix(tokens))
    order = order_matrix()
    forth, back = jnp.asarray(order), jnp.asarray(order.T)
    same_core = [[2 * chip + core for chip in range(chips)] for core in range(2)]
    cores = [(device, device ^ 1) for device in range(devices)]
    message_rows = experts * ROWS
    received_rows = chips * SLOTS

    other = [lax.ppermute(w[0], "ep", cores) for w in (w_gate, w_up, w_down)]
    mine = [w[0] for w in (w_gate, w_up, w_down)]

    params = pltpu.CompilerParams(vmem_limit_bytes=VMEM)

    def cost(flops, size):
        return pl.CostEstimate(flops=flops, bytes_accessed=size, transcendentals=0)

    packed_shape = jax.ShapeDtypeStruct((message_rows, part), bf16)
    stack = pltpu.VMEM((PARTS * tokens, part), bf16)
    pack_cost = cost(2 * message_rows * PARTS * tokens * part, 4 * tokens * width * 2)

    def exchange(rows):
        return lax.all_to_all(
            rows, "ep", split_axis=0, concat_axis=0, tiled=True, axis_index_groups=same_core
        )

    def run_experts(arrived):
        return pl.pallas_call(
            experts_kernel,
            out_shape=packed_shape,
            in_specs=[spec()] * 3 + [spec(pl.ANY)] * 6,
            out_specs=spec(),
            scratch_shapes=[
                pltpu.VMEM((PARTS, received_rows, part), bf16),
                pltpu.VMEM((DEPTH, part, 2 * half), bf16),
                pltpu.VMEM((PARTS, 2 * half, part), bf16),
                pltpu.VMEM((received_rows, 2 * half), f32),
                pltpu.VMEM((received_rows, 2 * half), bf16),
                pltpu.VMEM((received_rows // (GROUP * SLOTS), GROUP * ROWS, part), bf16),
                pltpu.SemaphoreType.DMA((DEPTH, 2)),
                pltpu.SemaphoreType.DMA((PARTS, 2)),
            ],
            compiler_params=params,
            cost_estimate=cost(12 * received_rows * width * half, 12 * width * half),
            name="experts",
        )(arrived, forth, back, *mine, *other)

    def run_combine(rows, weights, returned):
        return pl.pallas_call(
            combine,
            out_shape=jax.ShapeDtypeStruct((tokens, width), bf16),
            in_specs=[spec()] * 3,
            out_specs=spec(),
            compiler_params=params,
            cost_estimate=cost(4 * message_rows * PARTS * tokens * part, 5 * tokens * width * 2),
            name="combine",
        )(rows, weights, returned)

    packed = pl.pallas_call(
        functools.partial(first_pack, experts),
        out_shape=packed_shape,
        in_specs=[spec(pltpu.SMEM)] + [spec()] * 4,
        out_specs=spec(),
        scratch_shapes=[stack],
        compiler_params=params,
        cost_estimate=pack_cost,
        name="first_pack",
    )(order_of, own, gain, chosen, earlier)
    weights_shape = jax.ShapeDtypeStruct((2, PARTS * tokens, message_rows), bf16)
    send, first_weights, second_weights = pl.pallas_call(
        functools.partial(routing, experts, tokens),
        out_shape=(
            jax.ShapeDtypeStruct((message_rows, PARTS * tokens), bf16),
            weights_shape,
            weights_shape,
        ),
        in_specs=[spec(pltpu.SMEM)] + [spec()] * 3,
        out_specs=(spec(), spec(), spec()),
        compiler_params=params,
        cost_estimate=cost(message_rows * PARTS * tokens * 1000, 3 * message_rows * PARTS * tokens * 2),
        name="routing",
    )(order_of, chosen, gates, earlier)

    moved = run_combine(own, first_weights, exchange(run_experts(exchange(packed))))
    arrived = lax.ppermute(moved, "pp", [(0, 1), (1, 0)])
    packed = pl.pallas_call(
        second_pack,
        out_shape=packed_shape,
        in_specs=[spec()] * 3,
        out_specs=spec(),
        scratch_shapes=[stack],
        compiler_params=params,
        cost_estimate=pack_cost,
        name="second_pack",
    )(arrived, gain, send)
    finished = run_combine(arrived, second_weights, exchange(run_experts(exchange(packed))))
    return finished[None]


def solution(mesh):
    return jax.shard_map(
        shards,
        mesh=mesh,
        in_specs=(
            P("pp", "ep", None),
            P("pp", None),
            P("pp", None, "ep", None),
            P("pp", None, "ep", None),
            P("pp", None, "ep"),
            P("pp", None, "ep"),
            P("pp", "ep", None),
        ),
        out_specs=P("pp", "ep", None),
        check_vma=False,
    )
```

```python
import functools

import jax
import jax.numpy as jnp
import numpy as np
from jax import lax
from jax.experimental import pallas as pl
from jax.experimental.pallas import tpu as pltpu
from jax.sharding import PartitionSpec as P

EPS = 1e-06
SLOTS = 6
PARTS = 4
ROWS = SLOTS * PARTS
GROUP = 8
TAKE = GROUP * SLOTS
SIZE = GROUP * ROWS
AHEAD = 1
AHEAD_FLOPS = 20_000_000_000
INFO = 16
MIB = 1024 * 1024

f32 = jnp.float32
bf16 = jnp.bfloat16


def spec(space=pltpu.VMEM):
    return pl.BlockSpec(memory_space=space)


def to_bf16(condition):
    return jnp.where(condition, 1.0, 0.0).astype(bf16)


def earlier_matrix(tokens):
    size = PARTS * tokens
    a, b = np.arange(size)[:, None], np.arange(size)[None, :]
    return ((a // tokens == b // tokens) & (a % tokens < b % tokens)).astype(jnp.bfloat16)


def order_matrix():
    out = np.arange(SIZE)
    q, rest = out // TAKE, out % TAKE
    message, slot = rest // SLOTS, rest % SLOTS
    matrix = np.zeros((SIZE, SIZE), jnp.bfloat16)
    matrix[out, message * ROWS + q * SLOTS + slot] = 1
    return matrix


def spread_matrix(tokens):
    columns = np.arange(PARTS * tokens)
    return (np.arange(tokens)[:, None] == columns[None, :] % tokens).astype(np.float32)


def selection(routes, spread_ref, earlier_ref, tokens, experts):
    rows, columns = experts * ROWS, PARTS * tokens
    chosen = jnp.dot(routes, spread_ref[...], preferred_element_type=f32, precision=lax.Precision.HIGHEST)
    chosen = chosen.astype(jnp.int32)
    row = lax.broadcasted_iota(jnp.int32, (rows, 128), 0)
    expert = (row * 2731) >> 16
    rest = row - expert * ROWS
    piece = (rest * 43) >> 8
    slot = rest - piece * SLOTS
    wide = columns // 128
    expert, slot, piece = (jnp.concatenate([x] * wide, axis=1) for x in (expert, slot, piece))
    first = expert == chosen[0:1, :]
    named = jnp.logical_or(first, expert == chosen[1:2, :])
    before = jnp.dot(to_bf16(named), earlier_ref[...], preferred_element_type=f32)
    own = lax.broadcasted_iota(jnp.int32, (rows, columns), 1) // tokens
    fits = jnp.logical_and(before.astype(jnp.int32) == slot, piece == own)
    return jnp.logical_and(named, fits), first


def first_pack(
    experts, section_ref, tokens_ref, routes_ref, gates_ref, spread_ref, earlier_ref, out_ref, cross_ref, stack_ref
):
    tokens, width = tokens_ref.shape
    part = width // PARTS
    cross_ref[:tokens, :] = tokens_ref[:, width // 2 :]
    cross_ref[tokens:, :] = jnp.zeros((INFO, width // 2), bf16)
    rest = jnp.concatenate([gates_ref[0], gates_ref[1]], axis=0)
    info = [jnp.concatenate([routes_ref[0], routes_ref[1]], axis=0).astype(f32)]
    for _ in range(3):
        term = rest.astype(bf16).astype(f32)
        info.append(term)
        rest = rest - term
    cross_ref[tokens:, :tokens] = jnp.concatenate(info, axis=0).astype(bf16)
    routes = routes_ref[section_ref[0]].astype(f32)
    fills, _ = selection(routes, spread_ref, earlier_ref, tokens, experts)
    for q in range(PARTS):
        stack_ref[q * tokens : (q + 1) * tokens, :] = tokens_ref[:, q * part : (q + 1) * part]
    out_ref[...] = jnp.dot(to_bf16(fills), stack_ref[...], preferred_element_type=f32).astype(bf16)


def routing(
    experts, tokens, section_ref, own_routes, own_gates, cross_ref, spread_ref, earlier_ref,
    send_ref, first_ref, last_ref,
):
    section = section_ref[0]
    columns = PARTS * tokens

    info = cross_ref[:, :tokens].astype(f32)

    def of_other(micro):
        choices = [jnp.where(micro == 0, info[at : at + 2, :], info[at + 2 : at + 4, :]) for at in range(0, INFO, 4)]
        return choices[0], choices[1] + choices[2] + choices[3]

    def of_own(micro):
        return own_routes[micro].astype(f32), own_gates[micro]

    def put_weights(gates, fills, first, weights_ref, at):
        gates = jnp.dot(gates, spread_ref[...], preferred_element_type=f32, precision=lax.Precision.HIGHEST)
        scaled = jnp.where(fills, jnp.where(first, gates[0:1, :], gates[1:2, :]), 0.0).T
        high = scaled.astype(bf16)
        weights_ref[at, :columns, :] = high
        weights_ref[at, columns:, :] = (scaled - high.astype(f32)).astype(bf16)

    def select(routes):
        return selection(routes, spread_ref, earlier_ref, tokens, experts)

    routes, gates = of_own(section)
    put_weights(gates, *select(routes), first_ref, section)
    routes, gates = of_other(1 - section)
    put_weights(gates, *select(routes), first_ref, 1 - section)
    routes, _ = of_other(section)
    send_ref[1 - section] = to_bf16(select(routes)[0])
    routes, gates = of_own(1 - section)
    fills, first = select(routes)
    send_ref[section] = to_bf16(fills)
    put_weights(gates, fills, first, last_ref, 0)


def add_returned(weights, returned):
    both = jnp.dot(weights, returned, preferred_element_type=f32)
    half = both.shape[0] // 2
    return both[:half, :] + both[half:, :]


def turn(section_ref, own_ref, other_ref, weights_ref, returned_ref, send_ref, out_ref, kept_ref, came_ref, stack_ref):
    section = section_ref[0]
    tokens = own_ref.shape[0]
    lines, part = send_ref.shape[1], returned_ref.shape[1]
    for before_ref, after_ref, start, home, target in (
        (own_ref, kept_ref, 0, section, 1 - section),
        (other_ref, came_ref, 0, 1 - section, section),
    ):
        returned = returned_ref[pl.ds(pl.multiple_of(home * lines, lines), lines), :]
        added = add_returned(weights_ref[home], returned)
        for q in range(PARTS):
            rows, columns = slice(q * tokens, (q + 1) * tokens), slice(start + q * part, start + (q + 1) * part)
            value = (before_ref[:tokens, columns].astype(f32) + added[rows, :]).astype(bf16)
            after_ref[:, q * part : (q + 1) * part] = value
            stack_ref[rows, :] = value
        out_ref[pl.ds(pl.multiple_of(target * lines, lines), lines), :] = jnp.dot(
            send_ref[target], stack_ref[...], preferred_element_type=f32
        ).astype(bf16)


def combine(first_ref, second_ref, weights_ref, returned_ref, out_ref):
    tokens, width = out_ref.shape
    part = width // PARTS
    added = add_returned(weights_ref[0], returned_ref[...])
    for q in range(PARTS):
        source = first_ref if q < PARTS // 2 else second_ref
        at = (q % (PARTS // 2)) * part
        value = source[:, at : at + part].astype(f32) + added[q * tokens : (q + 1) * tokens, :]
        out_ref[:, q * part : (q + 1) * part] = value.astype(bf16)


def experts_kernel(
    crossed, section_ref, arrived_ref, gain_ref, order_ref, back_ref, g0, u0, d0, g1, u1, d1, out_ref,
    stack_ref, first_buf, second_buf, act_ref, hidden_ref, first_sem, second_sem,
):
    section = section_ref[0]
    rows, part = stack_ref.shape[1], stack_ref.shape[2]
    eighth = part // 2
    width = PARTS * part
    half = g0.shape[1]
    groups = rows // TAKE
    lines = groups * SIZE

    def columns_of(q):
        if crossed:
            return pl.ds(q * part, part)
        return pl.ds(pl.multiple_of((jnp.where(section == q // 2, 0, 2) + q % 2) * part, part), part)

    def load_first(q):
        return [
            pltpu.make_async_copy(
                source.at[pl.ds(q * part, part), :],
                first_buf.at[q, :, pl.ds(i * half, half)],
                first_sem.at[q, i],
            )
            for i, source in enumerate((g1, u1))
        ]

    def load_second(q):
        return [pltpu.make_async_copy(d1.at[:, columns_of(q)], second_buf.at[q], second_sem.at[q])]

    queue = [load_first(q) for q in range(PARTS)] + [load_second(q) for q in range(PARTS)]

    def wait(copies):
        for copy in copies:
            copy.wait()

    def start(copies):
        for copy in copies:
            copy.start()

    for copies in queue[:AHEAD]:
        start(copies)

    def wait(copies):
        for copy in copies:
            copy.wait()

    def reorder(at):
        return jnp.dot(order_ref[...], arrived_ref[pl.ds(at, SIZE), :], preferred_element_type=f32)

    def put_normed(at, pieces):
        total = sum(jnp.sum(piece * piece, axis=1, keepdims=True) for piece, _, _, _ in pieces)
        inverse = lax.rsqrt(total / width + EPS)
        for piece, quarter, column, gain in pieces:
            stack_ref[quarter, at : at + TAKE, column : column + piece.shape[1]] = (
                piece * inverse * gain
            ).astype(bf16)

    for group in range(groups):
        pieces = []
        if crossed:
            for side in range(2):
                home = 1 - section if side == 0 else section
                moved = reorder(pl.multiple_of(home * lines + group * SIZE, SIZE))
                for q in range(PARTS):
                    at = (side * PARTS + q) * eighth
                    pieces.append(
                        (moved[q * TAKE : (q + 1) * TAKE, :], 2 * side + q // 2, (q % 2) * eighth,
                         gain_ref[:, at : at + eighth])
                    )
        else:
            moved = reorder(group * SIZE)
            for q in range(PARTS):
                pieces.append(
                    (moved[q * TAKE : (q + 1) * TAKE, :], q, 0, gain_ref[:, q * part : (q + 1) * part])
                )
        put_normed(group * TAKE, pieces)

    def put_hidden(at):
        gate = act_ref[:, :half]
        value = gate / (1.0 + jnp.exp(-gate)) * act_ref[:, half:]
        hidden_ref[:, at : at + half] = value.astype(bf16)

    def add(q, at, product):
        if q == 0:
            act_ref[:, at : at + product.shape[1]] = product
        else:
            act_ref[:, at : at + product.shape[1]] += product

    for q in range(PARTS):
        for i, source in enumerate((g0, u0)):
            weights = source[q * part : (q + 1) * part, :]
            add(q, i * half, jnp.dot(stack_ref[q], weights, preferred_element_type=f32))
        start(queue[AHEAD + q])
    put_hidden(0)
    for q in range(PARTS):
        wait(queue[q])
        if AHEAD + PARTS + q < len(queue):
            start(queue[AHEAD + PARTS + q])
        add(q, 0, jnp.dot(stack_ref[q], first_buf[q], preferred_element_type=f32))
    put_hidden(half)
    for q in range(PARTS):
        wait(queue[PARTS + q])
        product = jnp.dot(hidden_ref[:, :half], d0[:, columns_of(q)], preferred_element_type=f32)
        product += jnp.dot(hidden_ref[:, half:], second_buf[q], preferred_element_type=f32)
        product = product.astype(bf16)
        for group in range(groups):
            piece = product[group * TAKE : (group + 1) * TAKE, :]
            if crossed:
                stack_ref[group, q * TAKE : (q + 1) * TAKE, :] = piece
            else:
                to = (q // 2) * eighth
                for i in range(2):
                    k = 2 * (q % 2) + i
                    stack_ref[group, k * TAKE : (k + 1) * TAKE, to : to + eighth] = piece[
                        :, i * eighth : (i + 1) * eighth
                    ]
        if not crossed and q % 2 == 1:
            to = (q // 2) * eighth
            for group in range(groups):
                at = ((q // 2) * groups + group) * SIZE
                out_ref[at : at + SIZE, :] = jnp.dot(
                    back_ref[...], stack_ref[group, :, to : to + eighth], preferred_element_type=f32
                ).astype(bf16)
    if crossed:
        for group in range(groups):
            out_ref[group * SIZE : (group + 1) * SIZE, :] = jnp.dot(
                back_ref[...], stack_ref[group], preferred_element_type=f32
            ).astype(bf16)


def shards(entering, norm_gain, routes, route_gates, w_gate, w_up, w_down):
    section = lax.axis_index("pp")
    devices = lax.axis_size("ep")
    chips = devices // 2
    experts = chips
    own = entering[0]
    tokens, width = own.shape
    part = width // PARTS
    side = width // 2
    half = w_gate.shape[2]
    lines = experts * ROWS
    received = chips * SLOTS
    columns = PARTS * tokens

    sections = [(0, 1), (1, 0)]
    cores = [(device, device ^ 1) for device in range(devices)]
    inside = [[2 * chip + core for chip in range(chips)] for core in range(2)]
    across = [[p * devices + 2 * chip + core for p in range(2) for chip in range(chips)] for core in range(2)]

    def exchange(rows, axes, groups):
        return lax.all_to_all(rows, axes, split_axis=0, concat_axis=0, tiled=True, axis_index_groups=groups)

    mine = [w[0] for w in (w_gate, w_up, w_down)]
    others = [lax.ppermute(w, "ep", cores) for w in mine]
    chosen = jnp.swapaxes(routes[0], 1, 2)
    gates = jnp.swapaxes(route_gates[0], 1, 2)

    at = section.astype(jnp.int32).reshape(1)
    spread = jnp.asarray(spread_matrix(tokens))
    earlier = jnp.asarray(earlier_matrix(tokens))
    order = order_matrix()
    forth, back = jnp.asarray(order), jnp.asarray(order.T)

    def near(x):
        return pltpu.with_memory_space_constraint(x, pltpu.VMEM)

    def far(x):
        return pltpu.with_memory_space_constraint(x, pltpu.HBM)

    def call(kernel, name, shapes, flops, size, limit, in_specs, scratch=()):
        return pl.pallas_call(
            kernel,
            out_shape=shapes,
            in_specs=in_specs,
            out_specs=tuple(spec() for _ in shapes) if isinstance(shapes, tuple) else spec(),
            scratch_shapes=list(scratch),
            compiler_params=pltpu.CompilerParams(vmem_limit_bytes=limit * MIB),
            cost_estimate=pl.CostEstimate(flops=flops, bytes_accessed=size, transcendentals=0),
            name=name,
        )

    scalar = spec(pltpu.SMEM)
    whole = jax.ShapeDtypeStruct((lines, part), bf16)
    halves = jax.ShapeDtypeStruct((2 * lines, part // 2), bf16)

    def run_experts(crossed, arrived):
        return call(
            functools.partial(experts_kernel, crossed),
            "experts",
            whole if crossed else halves,
            12 * received * width * half,
            12 * width * half,
            31,
            [scalar] + [spec()] * 7 + [spec(pl.ANY)] * 3,
            [
                pltpu.VMEM((PARTS, received, part), bf16),
                pltpu.VMEM((PARTS, part, 2 * half), bf16),
                pltpu.VMEM((PARTS, half, part), bf16),
                pltpu.VMEM((received, 2 * half), f32),
                pltpu.VMEM((received, 2 * half), bf16),
                pltpu.SemaphoreType.DMA((PARTS, 2)),
                pltpu.SemaphoreType.DMA((PARTS,)),
            ],
        )(at, near(arrived), norm_gain, forth, back, *[near(w) for w in mine], *others)

    packed, cross = call(
        functools.partial(first_pack, experts),
        "first_pack",
        (whole, jax.ShapeDtypeStruct((tokens + INFO, side), bf16)),
        AHEAD_FLOPS,
        4 * tokens * width * 2,
        16,
        [scalar] + [spec()] * 5,
        [pltpu.VMEM((columns, part), bf16)],
    )(at, far(own), far(chosen), far(gates), far(spread), far(earlier))
    arrived, cross = lax.optimization_barrier((exchange(packed, "ep", inside), cross))
    leaving, other = lax.optimization_barrier(
        (run_experts(False, arrived), lax.ppermute(cross, "pp", sections))
    )
    send, first_weights, last_weights = call(
        functools.partial(routing, experts, tokens),
        "routing",
        (
            jax.ShapeDtypeStruct((2, lines, columns), bf16),
            jax.ShapeDtypeStruct((2, 2 * columns, lines), bf16),
            jax.ShapeDtypeStruct((1, 2 * columns, lines), bf16),
        ),
        lines * columns * 4000,
        8 * lines * columns * 2,
        16,
        [scalar] + [spec()] * 5,
    )(at, chosen, gates, other[tokens:, :128], spread, earlier)

    returned = exchange(leaving, ("pp", "ep"), across)
    packed, kept, came = call(
        turn,
        "turn",
        (
            halves,
            pltpu.HBM((tokens, side), bf16),
            pltpu.HBM((tokens, side), bf16),
        ),
        AHEAD_FLOPS,
        8 * tokens * width * 2,
        16,
        [scalar] + [spec()] * 5,
        [pltpu.VMEM((columns, part // 2), bf16)],
    )(at, far(own), far(other), far(first_weights), near(returned), far(send))
    arrived = exchange(packed, ("pp", "ep"), across)
    kept, arrived = lax.optimization_barrier((kept, arrived))
    leaving, first_half = lax.optimization_barrier(
        (run_experts(True, arrived), lax.ppermute(kept, "pp", sections))
    )
    returned = exchange(leaving, "ep", inside)
    finished = call(
        combine,
        "combine",
        jax.ShapeDtypeStruct((tokens, width), bf16),
        4 * lines * columns * part,
        5 * tokens * width * 2,
        16,
        [spec()] * 4,
    )(first_half, came, last_weights, near(returned))
    return finished[None]


def solution(mesh):
    return jax.shard_map(
        shards,
        mesh=mesh,
        in_specs=(
            P("pp", "ep", None),
            P("pp", None),
            P("pp", None, "ep", None),
            P("pp", None, "ep", None),
            P("pp", None, "ep"),
            P("pp", None, "ep"),
            P("pp", "ep", None),
        ),
        out_specs=P("pp", "ep", None),
        check_vma=False,
    )
```

```python
import functools

import jax
import jax.numpy as jnp
import numpy as np
from jax import lax
from jax.experimental import pallas as pl
from jax.experimental.pallas import tpu as pltpu
from jax.sharding import PartitionSpec as P

EPS = 1e-06
SLOTS = 6
PARTS = 4
ROWS = SLOTS * PARTS
GROUP = 8
TAKE = GROUP * SLOTS
SIZE = GROUP * ROWS
AHEAD = 1
AHEAD_FLOPS = 20_000_000_000
INFO = 16
MIB = 1024 * 1024

f32 = jnp.float32
bf16 = jnp.bfloat16


def spec(space=pltpu.VMEM):
    return pl.BlockSpec(memory_space=space)


def to_bf16(condition):
    return jnp.where(condition, 1.0, 0.0).astype(bf16)


def chip_order():
    return [x * 8 + y * 4 + z for y in range(2) for x in range(4) for z in range(4)]


def place_on_path(chip):
    x, y, z = chip >> 3, jnp.bitwise_and(chip >> 2, 1), jnp.bitwise_and(chip, 3)
    return y * 16 + x * 4 + z


def earlier_matrix(tokens):
    size = PARTS * tokens
    a, b = np.arange(size)[:, None], np.arange(size)[None, :]
    return ((a // tokens == b // tokens) & (a % tokens < b % tokens)).astype(jnp.bfloat16)


def order_matrix():
    out = np.arange(SIZE)
    q, rest = out // TAKE, out % TAKE
    message, slot = rest // SLOTS, rest % SLOTS
    matrix = np.zeros((SIZE, SIZE), jnp.bfloat16)
    matrix[out, message * ROWS + q * SLOTS + slot] = 1
    return matrix


def spread_matrix(tokens):
    columns = np.arange(PARTS * tokens)
    return (np.arange(tokens)[:, None] == columns[None, :] % tokens).astype(np.float32)


def selection(routes, spread_ref, earlier_ref, tokens, experts):
    rows, columns = experts * ROWS, PARTS * tokens
    chosen = jnp.dot(routes, spread_ref[...], preferred_element_type=f32, precision=lax.Precision.HIGHEST)
    chosen = place_on_path(chosen.astype(jnp.int32))
    row = lax.broadcasted_iota(jnp.int32, (rows, 128), 0)
    expert = (row * 2731) >> 16
    rest = row - expert * ROWS
    piece = (rest * 43) >> 8
    slot = rest - piece * SLOTS
    wide = columns // 128
    expert, slot, piece = (jnp.concatenate([x] * wide, axis=1) for x in (expert, slot, piece))
    first = expert == chosen[0:1, :]
    named = jnp.logical_or(first, expert == chosen[1:2, :])
    before = jnp.dot(to_bf16(named), earlier_ref[...], preferred_element_type=f32)
    own = lax.broadcasted_iota(jnp.int32, (rows, columns), 1) // tokens
    fits = jnp.logical_and(before.astype(jnp.int32) == slot, piece == own)
    return jnp.logical_and(named, fits), first


def first_pack(
    experts, section_ref, tokens_ref, routes_ref, gates_ref, spread_ref, earlier_ref, out_ref, cross_ref, stack_ref
):
    tokens, width = tokens_ref.shape
    part = width // PARTS
    cross_ref[:tokens, :] = tokens_ref[:, width // 2 :]
    cross_ref[tokens:, :] = jnp.zeros((INFO, width // 2), bf16)
    rest = jnp.concatenate([gates_ref[0], gates_ref[1]], axis=0)
    info = [jnp.concatenate([routes_ref[0], routes_ref[1]], axis=0).astype(f32)]
    for _ in range(3):
        term = rest.astype(bf16).astype(f32)
        info.append(term)
        rest = rest - term
    cross_ref[tokens:, :tokens] = jnp.concatenate(info, axis=0).astype(bf16)
    routes = routes_ref[section_ref[0]].astype(f32)
    fills, _ = selection(routes, spread_ref, earlier_ref, tokens, experts)
    for q in range(PARTS):
        stack_ref[q * tokens : (q + 1) * tokens, :] = tokens_ref[:, q * part : (q + 1) * part]
    out_ref[...] = jnp.dot(to_bf16(fills), stack_ref[...], preferred_element_type=f32).astype(bf16)


def routing(
    experts, tokens, section_ref, own_routes, own_gates, cross_ref, spread_ref, earlier_ref,
    send_ref, first_ref, last_ref,
):
    section = section_ref[0]
    columns = PARTS * tokens

    info = cross_ref[:, :tokens].astype(f32)

    def of_other(micro):
        choices = [jnp.where(micro == 0, info[at : at + 2, :], info[at + 2 : at + 4, :]) for at in range(0, INFO, 4)]
        return choices[0], choices[1] + choices[2] + choices[3]

    def of_own(micro):
        return own_routes[micro].astype(f32), own_gates[micro]

    def put_weights(gates, fills, first, weights_ref, at):
        gates = jnp.dot(gates, spread_ref[...], preferred_element_type=f32, precision=lax.Precision.HIGHEST)
        scaled = jnp.where(fills, jnp.where(first, gates[0:1, :], gates[1:2, :]), 0.0).T
        high = scaled.astype(bf16)
        weights_ref[at, :columns, :] = high
        weights_ref[at, columns:, :] = (scaled - high.astype(f32)).astype(bf16)

    def select(routes):
        return selection(routes, spread_ref, earlier_ref, tokens, experts)

    routes, gates = of_own(section)
    put_weights(gates, *select(routes), first_ref, section)
    routes, gates = of_other(1 - section)
    put_weights(gates, *select(routes), first_ref, 1 - section)
    routes, _ = of_other(section)
    send_ref[1 - section] = to_bf16(select(routes)[0])
    routes, gates = of_own(1 - section)
    fills, first = select(routes)
    send_ref[section] = to_bf16(fills)
    put_weights(gates, fills, first, last_ref, 0)


def add_returned(weights, returned):
    both = jnp.dot(weights, returned, preferred_element_type=f32)
    half = both.shape[0] // 2
    return both[:half, :] + both[half:, :]


def turn(section_ref, own_ref, other_ref, weights_ref, returned_ref, send_ref, out_ref, kept_ref, came_ref, stack_ref):
    section = section_ref[0]
    tokens = own_ref.shape[0]
    lines, part = send_ref.shape[1], returned_ref.shape[1]
    for before_ref, after_ref, start, home, target in (
        (own_ref, kept_ref, 0, section, 1 - section),
        (other_ref, came_ref, 0, 1 - section, section),
    ):
        returned = returned_ref[pl.ds(pl.multiple_of(home * lines, lines), lines), :]
        added = add_returned(weights_ref[home], returned)
        for q in range(PARTS):
            rows, columns = slice(q * tokens, (q + 1) * tokens), slice(start + q * part, start + (q + 1) * part)
            value = (before_ref[:tokens, columns].astype(f32) + added[rows, :]).astype(bf16)
            after_ref[:, q * part : (q + 1) * part] = value
            stack_ref[rows, :] = value
        out_ref[pl.ds(pl.multiple_of(target * lines, lines), lines), :] = jnp.dot(
            send_ref[target], stack_ref[...], preferred_element_type=f32
        ).astype(bf16)


def combine(first_ref, second_ref, weights_ref, returned_ref, out_ref):
    tokens, width = out_ref.shape
    part = width // PARTS
    added = add_returned(weights_ref[0], returned_ref[...])
    for q in range(PARTS):
        source = first_ref if q < PARTS // 2 else second_ref
        at = (q % (PARTS // 2)) * part
        value = source[:, at : at + part].astype(f32) + added[q * tokens : (q + 1) * tokens, :]
        out_ref[:, q * part : (q + 1) * part] = value.astype(bf16)


def experts_kernel(
    crossed, section_ref, arrived_ref, gain_ref, order_ref, back_ref, g0, u0, d0, g1, u1, d1, out_ref,
    stack_ref, first_buf, second_buf, act_ref, hidden_ref, first_sem, second_sem,
):
    section = section_ref[0]
    rows, part = stack_ref.shape[1], stack_ref.shape[2]
    eighth = part // 2
    width = PARTS * part
    half = g0.shape[1]
    groups = rows // TAKE
    lines = groups * SIZE

    def columns_of(q):
        if crossed:
            return pl.ds(q * part, part)
        return pl.ds(pl.multiple_of((jnp.where(section == q // 2, 0, 2) + q % 2) * part, part), part)

    def load_first(q):
        return [
            pltpu.make_async_copy(
                source.at[pl.ds(q * part, part), :],
                first_buf.at[q, :, pl.ds(i * half, half)],
                first_sem.at[q, i],
            )
            for i, source in enumerate((g1, u1))
        ]

    def load_second(q):
        return [pltpu.make_async_copy(d1.at[:, columns_of(q)], second_buf.at[q], second_sem.at[q])]

    queue = [load_first(q) for q in range(PARTS)] + [load_second(q) for q in range(PARTS)]

    def wait(copies):
        for copy in copies:
            copy.wait()

    def start(copies):
        for copy in copies:
            copy.start()

    for copies in queue[:AHEAD]:
        start(copies)

    def wait(copies):
        for copy in copies:
            copy.wait()

    def reorder(at):
        return jnp.dot(order_ref[...], arrived_ref[pl.ds(at, SIZE), :], preferred_element_type=f32)

    def put_normed(at, pieces):
        total = sum(jnp.sum(piece * piece, axis=1, keepdims=True) for piece, _, _, _ in pieces)
        inverse = lax.rsqrt(total / width + EPS)
        for piece, quarter, column, gain in pieces:
            stack_ref[quarter, at : at + TAKE, column : column + piece.shape[1]] = (
                piece * inverse * gain
            ).astype(bf16)

    for group in range(groups):
        pieces = []
        if crossed:
            for side in range(2):
                home = 1 - section if side == 0 else section
                moved = reorder(pl.multiple_of(home * lines + group * SIZE, SIZE))
                for q in range(PARTS):
                    at = (side * PARTS + q) * eighth
                    pieces.append(
                        (moved[q * TAKE : (q + 1) * TAKE, :], 2 * side + q // 2, (q % 2) * eighth,
                         gain_ref[:, at : at + eighth])
                    )
        else:
            moved = reorder(group * SIZE)
            for q in range(PARTS):
                pieces.append(
                    (moved[q * TAKE : (q + 1) * TAKE, :], q, 0, gain_ref[:, q * part : (q + 1) * part])
                )
        put_normed(group * TAKE, pieces)

    def put_hidden(at):
        gate = act_ref[:, :half]
        value = gate / (1.0 + jnp.exp(-gate)) * act_ref[:, half:]
        hidden_ref[:, at : at + half] = value.astype(bf16)

    def add(q, at, product):
        if q == 0:
            act_ref[:, at : at + product.shape[1]] = product
        else:
            act_ref[:, at : at + product.shape[1]] += product

    for q in range(PARTS):
        for i, source in enumerate((g0, u0)):
            weights = source[q * part : (q + 1) * part, :]
            add(q, i * half, jnp.dot(stack_ref[q], weights, preferred_element_type=f32))
        start(queue[AHEAD + q])
    put_hidden(0)
    for q in range(PARTS):
        wait(queue[q])
        if AHEAD + PARTS + q < len(queue):
            start(queue[AHEAD + PARTS + q])
        add(q, 0, jnp.dot(stack_ref[q], first_buf[q], preferred_element_type=f32))
    put_hidden(half)
    for q in range(PARTS):
        wait(queue[PARTS + q])
        product = jnp.dot(hidden_ref[:, :half], d0[:, columns_of(q)], preferred_element_type=f32)
        product += jnp.dot(hidden_ref[:, half:], second_buf[q], preferred_element_type=f32)
        product = product.astype(bf16)
        for group in range(groups):
            piece = product[group * TAKE : (group + 1) * TAKE, :]
            if crossed:
                stack_ref[group, q * TAKE : (q + 1) * TAKE, :] = piece
            else:
                to = (q // 2) * eighth
                for i in range(2):
                    k = 2 * (q % 2) + i
                    stack_ref[group, k * TAKE : (k + 1) * TAKE, to : to + eighth] = piece[
                        :, i * eighth : (i + 1) * eighth
                    ]
        if not crossed and q % 2 == 1:
            to = (q // 2) * eighth
            for group in range(groups):
                at = ((q // 2) * groups + group) * SIZE
                out_ref[at : at + SIZE, :] = jnp.dot(
                    back_ref[...], stack_ref[group, :, to : to + eighth], preferred_element_type=f32
                ).astype(bf16)
    if crossed:
        for group in range(groups):
            out_ref[group * SIZE : (group + 1) * SIZE, :] = jnp.dot(
                back_ref[...], stack_ref[group], preferred_element_type=f32
            ).astype(bf16)


def shards(entering, norm_gain, routes, route_gates, w_gate, w_up, w_down):
    section = lax.axis_index("pp")
    devices = lax.axis_size("ep")
    chips = devices // 2
    experts = chips
    own = entering[0]
    tokens, width = own.shape
    part = width // PARTS
    side = width // 2
    half = w_gate.shape[2]
    lines = experts * ROWS
    received = chips * SLOTS
    columns = PARTS * tokens

    sections = [(0, 1), (1, 0)]
    cores = [(device, device ^ 1) for device in range(devices)]
    inside = [[2 * chip + core for chip in chip_order()] for core in range(2)]
    across = [[p * devices + 2 * chip + core for p in range(2) for chip in chip_order()] for core in range(2)]

    def exchange(rows, axes, groups):
        return lax.all_to_all(rows, axes, split_axis=0, concat_axis=0, tiled=True, axis_index_groups=groups)

    mine = [w[0] for w in (w_gate, w_up, w_down)]
    others = [lax.ppermute(w, "ep", cores) for w in mine]
    chosen = jnp.swapaxes(routes[0], 1, 2)
    gates = jnp.swapaxes(route_gates[0], 1, 2)

    at = section.astype(jnp.int32).reshape(1)
    spread = jnp.asarray(spread_matrix(tokens))
    earlier = jnp.asarray(earlier_matrix(tokens))
    order = order_matrix()
    forth, back = jnp.asarray(order), jnp.asarray(order.T)

    def near(x):
        return pltpu.with_memory_space_constraint(x, pltpu.VMEM)

    def far(x):
        return pltpu.with_memory_space_constraint(x, pltpu.HBM)

    def call(kernel, name, shapes, flops, size, limit, in_specs, scratch=()):
        return pl.pallas_call(
            kernel,
            out_shape=shapes,
            in_specs=in_specs,
            out_specs=tuple(spec() for _ in shapes) if isinstance(shapes, tuple) else spec(),
            scratch_shapes=list(scratch),
            compiler_params=pltpu.CompilerParams(vmem_limit_bytes=limit * MIB),
            cost_estimate=pl.CostEstimate(flops=flops, bytes_accessed=size, transcendentals=0),
            name=name,
        )

    scalar = spec(pltpu.SMEM)
    whole = jax.ShapeDtypeStruct((lines, part), bf16)
    halves = jax.ShapeDtypeStruct((2 * lines, part // 2), bf16)

    def run_experts(crossed, arrived):
        return call(
            functools.partial(experts_kernel, crossed),
            "experts",
            whole if crossed else halves,
            12 * received * width * half,
            12 * width * half,
            31,
            [scalar] + [spec()] * 7 + [spec(pl.ANY)] * 3,
            [
                pltpu.VMEM((PARTS, received, part), bf16),
                pltpu.VMEM((PARTS, part, 2 * half), bf16),
                pltpu.VMEM((PARTS, half, part), bf16),
                pltpu.VMEM((received, 2 * half), f32),
                pltpu.VMEM((received, 2 * half), bf16),
                pltpu.SemaphoreType.DMA((PARTS, 2)),
                pltpu.SemaphoreType.DMA((PARTS,)),
            ],
        )(at, near(arrived), norm_gain, forth, back, *[near(w) for w in mine], *others)

    packed, cross = call(
        functools.partial(first_pack, experts),
        "first_pack",
        (whole, jax.ShapeDtypeStruct((tokens + INFO, side), bf16)),
        AHEAD_FLOPS,
        4 * tokens * width * 2,
        16,
        [scalar] + [spec()] * 5,
        [pltpu.VMEM((columns, part), bf16)],
    )(at, far(own), far(chosen), far(gates), far(spread), far(earlier))
    arrived, cross = lax.optimization_barrier((exchange(packed, "ep", inside), cross))
    leaving, other = lax.optimization_barrier(
        (run_experts(False, arrived), lax.ppermute(cross, "pp", sections))
    )
    send, first_weights, last_weights = call(
        functools.partial(routing, experts, tokens),
        "routing",
        (
            jax.ShapeDtypeStruct((2, lines, columns), bf16),
            jax.ShapeDtypeStruct((2, 2 * columns, lines), bf16),
            jax.ShapeDtypeStruct((1, 2 * columns, lines), bf16),
        ),
        lines * columns * 4000,
        8 * lines * columns * 2,
        16,
        [scalar] + [spec()] * 5,
    )(at, chosen, gates, other[tokens:, :128], spread, earlier)

    returned = exchange(leaving, ("pp", "ep"), across)
    packed, kept, came = call(
        turn,
        "turn",
        (
            halves,
            pltpu.HBM((tokens, side), bf16),
            pltpu.HBM((tokens, side), bf16),
        ),
        AHEAD_FLOPS,
        8 * tokens * width * 2,
        16,
        [scalar] + [spec()] * 5,
        [pltpu.VMEM((columns, part // 2), bf16)],
    )(at, far(own), far(other), far(first_weights), near(returned), far(send))
    arrived = exchange(packed, ("pp", "ep"), across)
    kept, arrived = lax.optimization_barrier((kept, arrived))
    leaving, first_half = lax.optimization_barrier(
        (run_experts(True, arrived), lax.ppermute(kept, "pp", sections))
    )
    returned = exchange(leaving, "ep", inside)
    finished = call(
        combine,
        "combine",
        jax.ShapeDtypeStruct((tokens, width), bf16),
        4 * lines * columns * part,
        5 * tokens * width * 2,
        16,
        [spec()] * 4,
    )(first_half, came, last_weights, near(returned))
    return finished[None]


def solution(mesh):
    return jax.shard_map(
        shards,
        mesh=mesh,
        in_specs=(
            P("pp", "ep", None),
            P("pp", None),
            P("pp", None, "ep", None),
            P("pp", None, "ep", None),
            P("pp", None, "ep"),
            P("pp", None, "ep"),
            P("pp", "ep", None),
        ),
        out_specs=P("pp", "ep", None),
        check_vma=False,
    )
```

```python
import functools

import jax
import jax.numpy as jnp
import numpy as np
from jax import lax
from jax.experimental import pallas as pl
from jax.experimental.pallas import tpu as pltpu
from jax.sharding import PartitionSpec as P

EPS = 1e-06
SLOTS = 6
PARTS = 4
ROWS = SLOTS * PARTS
GROUP = 8
TAKE = GROUP * SLOTS
SIZE = GROUP * ROWS
AHEAD = 0
AHEAD_FLOPS = 20_000_000_000
INFO = 16
MIB = 1024 * 1024

f32 = jnp.float32
bf16 = jnp.bfloat16


def spec(space=pltpu.VMEM):
    return pl.BlockSpec(memory_space=space)


def to_bf16(condition):
    return jnp.where(condition, 1.0, 0.0).astype(bf16)


def chip_order():
    return [x * 8 + y * 4 + z for y in range(2) for x in range(4) for z in range(4)]


def place_on_path(chip):
    x, y, z = chip >> 3, jnp.bitwise_and(chip >> 2, 1), jnp.bitwise_and(chip, 3)
    return y * 16 + x * 4 + z


def earlier_matrix(tokens):
    size = PARTS * tokens
    a, b = np.arange(size)[:, None], np.arange(size)[None, :]
    return ((a // tokens == b // tokens) & (a % tokens < b % tokens)).astype(jnp.bfloat16)


def order_matrix():
    out = np.arange(SIZE)
    q, rest = out // TAKE, out % TAKE
    message, slot = rest // SLOTS, rest % SLOTS
    matrix = np.zeros((SIZE, SIZE), jnp.bfloat16)
    matrix[out, message * ROWS + q * SLOTS + slot] = 1
    return matrix


def spread_matrix(tokens):
    columns = np.arange(PARTS * tokens)
    return (np.arange(tokens)[:, None] == columns[None, :] % tokens).astype(np.float32)


def selection(routes, spread_ref, earlier_ref, tokens, experts):
    rows, columns = experts * ROWS, PARTS * tokens
    chosen = jnp.dot(routes, spread_ref[...], preferred_element_type=f32, precision=lax.Precision.HIGHEST)
    chosen = place_on_path(chosen.astype(jnp.int32))
    row = lax.broadcasted_iota(jnp.int32, (rows, 128), 0)
    expert = (row * 2731) >> 16
    rest = row - expert * ROWS
    piece = (rest * 43) >> 8
    slot = rest - piece * SLOTS
    wide = columns // 128
    expert, slot, piece = (jnp.concatenate([x] * wide, axis=1) for x in (expert, slot, piece))
    first = expert == chosen[0:1, :]
    named = jnp.logical_or(first, expert == chosen[1:2, :])
    before = jnp.dot(to_bf16(named), earlier_ref[...], preferred_element_type=f32)
    own = lax.broadcasted_iota(jnp.int32, (rows, columns), 1) // tokens
    fits = jnp.logical_and(before.astype(jnp.int32) == slot, piece == own)
    return jnp.logical_and(named, fits), first


def first_pack(
    experts, section_ref, tokens_ref, routes_ref, gates_ref, spread_ref, earlier_ref, out_ref, cross_ref, stack_ref
):
    tokens, width = tokens_ref.shape
    part = width // PARTS
    cross_ref[:tokens, :] = tokens_ref[:, width // 2 :]
    cross_ref[tokens:, :] = jnp.zeros((INFO, width // 2), bf16)
    rest = jnp.concatenate([gates_ref[0], gates_ref[1]], axis=0)
    info = [jnp.concatenate([routes_ref[0], routes_ref[1]], axis=0).astype(f32)]
    for _ in range(3):
        term = rest.astype(bf16).astype(f32)
        info.append(term)
        rest = rest - term
    cross_ref[tokens:, :tokens] = jnp.concatenate(info, axis=0).astype(bf16)
    routes = routes_ref[section_ref[0]].astype(f32)
    fills, _ = selection(routes, spread_ref, earlier_ref, tokens, experts)
    for q in range(PARTS):
        stack_ref[q * tokens : (q + 1) * tokens, :] = tokens_ref[:, q * part : (q + 1) * part]
    out_ref[...] = jnp.dot(to_bf16(fills), stack_ref[...], preferred_element_type=f32).astype(bf16)


def routing(
    experts, tokens, section_ref, own_routes, own_gates, cross_ref, spread_ref, earlier_ref,
    send_ref, first_ref, last_ref,
):
    section = section_ref[0]
    columns = PARTS * tokens

    info = cross_ref[:, :tokens].astype(f32)

    def of_other(micro):
        choices = [jnp.where(micro == 0, info[at : at + 2, :], info[at + 2 : at + 4, :]) for at in range(0, INFO, 4)]
        return choices[0], choices[1] + choices[2] + choices[3]

    def of_own(micro):
        return own_routes[micro].astype(f32), own_gates[micro]

    def put_weights(gates, fills, first, weights_ref, at):
        gates = jnp.dot(gates, spread_ref[...], preferred_element_type=f32, precision=lax.Precision.HIGHEST)
        scaled = jnp.where(fills, jnp.where(first, gates[0:1, :], gates[1:2, :]), 0.0).T
        high = scaled.astype(bf16)
        weights_ref[at, :columns, :] = high
        weights_ref[at, columns:, :] = (scaled - high.astype(f32)).astype(bf16)

    def select(routes):
        return selection(routes, spread_ref, earlier_ref, tokens, experts)

    routes, gates = of_own(section)
    put_weights(gates, *select(routes), first_ref, section)
    routes, gates = of_other(1 - section)
    put_weights(gates, *select(routes), first_ref, 1 - section)
    routes, _ = of_other(section)
    send_ref[1 - section] = to_bf16(select(routes)[0])
    routes, gates = of_own(1 - section)
    fills, first = select(routes)
    send_ref[section] = to_bf16(fills)
    put_weights(gates, fills, first, last_ref, 0)


def add_returned(weights, returned):
    both = jnp.dot(weights, returned, preferred_element_type=f32)
    half = both.shape[0] // 2
    return both[:half, :] + both[half:, :]


def turn(section_ref, own_ref, other_ref, weights_ref, returned_ref, send_ref, out_ref, kept_ref, came_ref, stack_ref):
    section = section_ref[0]
    tokens = own_ref.shape[0]
    lines, part = send_ref.shape[1], returned_ref.shape[1]
    for before_ref, after_ref, start, home, target in (
        (own_ref, kept_ref, 0, section, 1 - section),
        (other_ref, came_ref, 0, 1 - section, section),
    ):
        returned = returned_ref[pl.ds(pl.multiple_of(home * lines, lines), lines), :]
        added = add_returned(weights_ref[home], returned)
        for q in range(PARTS):
            rows, columns = slice(q * tokens, (q + 1) * tokens), slice(start + q * part, start + (q + 1) * part)
            value = (before_ref[:tokens, columns].astype(f32) + added[rows, :]).astype(bf16)
            after_ref[:, q * part : (q + 1) * part] = value
            stack_ref[rows, :] = value
        out_ref[pl.ds(pl.multiple_of(target * lines, lines), lines), :] = jnp.dot(
            send_ref[target], stack_ref[...], preferred_element_type=f32
        ).astype(bf16)


def combine(first_ref, second_ref, weights_ref, returned_ref, out_ref):
    tokens, width = out_ref.shape
    part = width // PARTS
    added = add_returned(weights_ref[0], returned_ref[...])
    for q in range(PARTS):
        source = first_ref if q < PARTS // 2 else second_ref
        at = (q % (PARTS // 2)) * part
        value = source[:, at : at + part].astype(f32) + added[q * tokens : (q + 1) * tokens, :]
        out_ref[:, q * part : (q + 1) * part] = value.astype(bf16)


def experts_kernel(
    crossed, section_ref, arrived_ref, gain_ref, order_ref, back_ref, g0, u0, d0, g1, u1, d1, out_ref,
    stack_ref, first_buf, second_buf, act_ref, hidden_ref, first_sem, second_sem,
):
    section = section_ref[0]
    rows, part = stack_ref.shape[1], stack_ref.shape[2]
    eighth = part // 2
    width = PARTS * part
    half = g0.shape[1]
    groups = rows // TAKE
    lines = groups * SIZE

    def columns_of(q):
        if crossed:
            return pl.ds(q * part, part)
        return pl.ds(pl.multiple_of((jnp.where(section == q // 2, 0, 2) + q % 2) * part, part), part)

    def load_first(q):
        return [
            pltpu.make_async_copy(
                source.at[pl.ds(q * part, part), :],
                first_buf.at[q, :, pl.ds(i * half, half)],
                first_sem.at[q, i],
            )
            for i, source in enumerate((g1, u1))
        ]

    def load_second(q):
        return [pltpu.make_async_copy(d1.at[:, columns_of(q)], second_buf.at[q], second_sem.at[q])]

    queue = [load_first(q) for q in range(PARTS)] + [load_second(q) for q in range(PARTS)]

    def wait(copies):
        for copy in copies:
            copy.wait()

    def start(copies):
        for copy in copies:
            copy.start()

    for copies in queue[:AHEAD]:
        start(copies)

    def wait(copies):
        for copy in copies:
            copy.wait()

    def reorder(at):
        return jnp.dot(order_ref[...], arrived_ref[pl.ds(at, SIZE), :], preferred_element_type=f32)

    def put_normed(at, pieces):
        total = sum(jnp.sum(piece * piece, axis=1, keepdims=True) for piece, _, _, _ in pieces)
        inverse = lax.rsqrt(total / width + EPS)
        for piece, quarter, column, gain in pieces:
            stack_ref[quarter, at : at + TAKE, column : column + piece.shape[1]] = (
                piece * inverse * gain
            ).astype(bf16)

    for group in range(groups):
        pieces = []
        if crossed:
            for side in range(2):
                home = 1 - section if side == 0 else section
                moved = reorder(pl.multiple_of(home * lines + group * SIZE, SIZE))
                for q in range(PARTS):
                    at = (side * PARTS + q) * eighth
                    pieces.append(
                        (moved[q * TAKE : (q + 1) * TAKE, :], 2 * side + q // 2, (q % 2) * eighth,
                         gain_ref[:, at : at + eighth])
                    )
        else:
            moved = reorder(group * SIZE)
            for q in range(PARTS):
                pieces.append(
                    (moved[q * TAKE : (q + 1) * TAKE, :], q, 0, gain_ref[:, q * part : (q + 1) * part])
                )
        put_normed(group * TAKE, pieces)

    def put_hidden(at):
        gate = act_ref[:, :half]
        value = gate / (1.0 + jnp.exp(-gate)) * act_ref[:, half:]
        hidden_ref[:, at : at + half] = value.astype(bf16)

    def add(q, at, product):
        if q == 0:
            act_ref[:, at : at + product.shape[1]] = product
        else:
            act_ref[:, at : at + product.shape[1]] += product

    for q in range(PARTS):
        for i, source in enumerate((g0, u0)):
            weights = source[q * part : (q + 1) * part, :]
            add(q, i * half, jnp.dot(stack_ref[q], weights, preferred_element_type=f32))
        start(queue[AHEAD + q])
    put_hidden(0)
    for q in range(PARTS):
        wait(queue[q])
        if AHEAD + PARTS + q < len(queue):
            start(queue[AHEAD + PARTS + q])
        add(q, 0, jnp.dot(stack_ref[q], first_buf[q], preferred_element_type=f32))
    put_hidden(half)
    for q in range(PARTS):
        wait(queue[PARTS + q])
        product = jnp.dot(hidden_ref[:, :half], d0[:, columns_of(q)], preferred_element_type=f32)
        product += jnp.dot(hidden_ref[:, half:], second_buf[q], preferred_element_type=f32)
        product = product.astype(bf16)
        for group in range(groups):
            piece = product[group * TAKE : (group + 1) * TAKE, :]
            if crossed:
                stack_ref[group, q * TAKE : (q + 1) * TAKE, :] = piece
            else:
                to = (q // 2) * eighth
                for i in range(2):
                    k = 2 * (q % 2) + i
                    stack_ref[group, k * TAKE : (k + 1) * TAKE, to : to + eighth] = piece[
                        :, i * eighth : (i + 1) * eighth
                    ]
        if not crossed and q % 2 == 1:
            to = (q // 2) * eighth
            for group in range(groups):
                at = ((q // 2) * groups + group) * SIZE
                out_ref[at : at + SIZE, :] = jnp.dot(
                    back_ref[...], stack_ref[group, :, to : to + eighth], preferred_element_type=f32
                ).astype(bf16)
    if crossed:
        for group in range(groups):
            out_ref[group * SIZE : (group + 1) * SIZE, :] = jnp.dot(
                back_ref[...], stack_ref[group], preferred_element_type=f32
            ).astype(bf16)


def shards(entering, norm_gain, routes, route_gates, w_gate, w_up, w_down):
    section = lax.axis_index("pp")
    devices = lax.axis_size("ep")
    chips = devices // 2
    experts = chips
    own = entering[0]
    tokens, width = own.shape
    part = width // PARTS
    side = width // 2
    half = w_gate.shape[2]
    lines = experts * ROWS
    received = chips * SLOTS
    columns = PARTS * tokens

    sections = [(0, 1), (1, 0)]
    cores = [(device, device ^ 1) for device in range(devices)]
    inside = [[2 * chip + core for chip in chip_order()] for core in range(2)]
    across = [[p * devices + 2 * chip + core for p in range(2) for chip in chip_order()] for core in range(2)]

    def exchange(rows, axes, groups):
        return lax.all_to_all(rows, axes, split_axis=0, concat_axis=0, tiled=True, axis_index_groups=groups)

    mine = [w[0] for w in (w_gate, w_up, w_down)]
    others = [lax.ppermute(w, "ep", cores) for w in mine]
    chosen = jnp.swapaxes(routes[0], 1, 2)
    gates = jnp.swapaxes(route_gates[0], 1, 2)

    at = section.astype(jnp.int32).reshape(1)
    spread = jnp.asarray(spread_matrix(tokens))
    earlier = jnp.asarray(earlier_matrix(tokens))
    order = order_matrix()
    forth, back = jnp.asarray(order), jnp.asarray(order.T)

    def near(x):
        return pltpu.with_memory_space_constraint(x, pltpu.VMEM)

    def far(x):
        return pltpu.with_memory_space_constraint(x, pltpu.HBM)

    def call(kernel, name, shapes, flops, size, limit, in_specs, scratch=()):
        return pl.pallas_call(
            kernel,
            out_shape=shapes,
            in_specs=in_specs,
            out_specs=tuple(spec() for _ in shapes) if isinstance(shapes, tuple) else spec(),
            scratch_shapes=list(scratch),
            compiler_params=pltpu.CompilerParams(vmem_limit_bytes=limit * MIB),
            cost_estimate=pl.CostEstimate(flops=flops, bytes_accessed=size, transcendentals=0),
            name=name,
        )

    scalar = spec(pltpu.SMEM)
    whole = jax.ShapeDtypeStruct((lines, part), bf16)
    halves = jax.ShapeDtypeStruct((2 * lines, part // 2), bf16)

    def run_experts(crossed, arrived):
        return call(
            functools.partial(experts_kernel, crossed),
            "experts",
            whole if crossed else halves,
            12 * received * width * half,
            12 * width * half,
            31,
            [scalar] + [spec()] * 7 + [spec(pl.ANY)] * 3,
            [
                pltpu.VMEM((PARTS, received, part), bf16),
                pltpu.VMEM((PARTS, part, 2 * half), bf16),
                pltpu.VMEM((PARTS, half, part), bf16),
                pltpu.VMEM((received, 2 * half), f32),
                pltpu.VMEM((received, 2 * half), bf16),
                pltpu.SemaphoreType.DMA((PARTS, 2)),
                pltpu.SemaphoreType.DMA((PARTS,)),
            ],
        )(at, near(arrived), norm_gain, forth, back, *[near(w) for w in mine], *others)

    packed, cross = call(
        functools.partial(first_pack, experts),
        "first_pack",
        (whole, jax.ShapeDtypeStruct((tokens + INFO, side), bf16)),
        AHEAD_FLOPS,
        4 * tokens * width * 2,
        16,
        [scalar] + [spec()] * 5,
        [pltpu.VMEM((columns, part), bf16)],
    )(at, far(own), far(chosen), far(gates), far(spread), far(earlier))
    arrived, cross = lax.optimization_barrier((exchange(packed, "ep", inside), cross))
    leaving, other = lax.optimization_barrier(
        (run_experts(False, arrived), lax.ppermute(cross, "pp", sections))
    )
    send, first_weights, last_weights = call(
        functools.partial(routing, experts, tokens),
        "routing",
        (
            jax.ShapeDtypeStruct((2, lines, columns), bf16),
            jax.ShapeDtypeStruct((2, 2 * columns, lines), bf16),
            jax.ShapeDtypeStruct((1, 2 * columns, lines), bf16),
        ),
        lines * columns * 4000,
        8 * lines * columns * 2,
        16,
        [scalar] + [spec()] * 5,
    )(at, chosen, gates, other[tokens:, :128], spread, earlier)

    returned = exchange(leaving, ("pp", "ep"), across)
    packed, kept, came = call(
        turn,
        "turn",
        (
            halves,
            pltpu.HBM((tokens, side), bf16),
            pltpu.HBM((tokens, side), bf16),
        ),
        AHEAD_FLOPS,
        8 * tokens * width * 2,
        16,
        [scalar] + [spec()] * 5,
        [pltpu.VMEM((columns, part // 2), bf16)],
    )(at, far(own), far(other), far(first_weights), near(returned), far(send))
    arrived = exchange(packed, ("pp", "ep"), across)
    kept, arrived = lax.optimization_barrier((kept, arrived))
    leaving, first_half = lax.optimization_barrier(
        (run_experts(True, arrived), lax.ppermute(kept, "pp", sections))
    )
    returned = exchange(leaving, "ep", inside)
    finished = call(
        combine,
        "combine",
        jax.ShapeDtypeStruct((tokens, width), bf16),
        4 * lines * columns * part,
        5 * tokens * width * 2,
        16,
        [spec()] * 4,
    )(first_half, came, last_weights, near(returned))
    return finished[None]


def solution(mesh):
    return jax.shard_map(
        shards,
        mesh=mesh,
        in_specs=(
            P("pp", "ep", None),
            P("pp", None),
            P("pp", None, "ep", None),
            P("pp", None, "ep", None),
            P("pp", None, "ep"),
            P("pp", None, "ep"),
            P("pp", "ep", None),
        ),
        out_specs=P("pp", "ep", None),
        check_vma=False,
    )
```
